32 devices in a mesh: frame: 4 (over y, x), vox: 8 (over z, core).
Axes of the slice: x: 2, y: 2, z: 4, core: 2. Of those that a mesh axis runs over, the one named last changes fastest.
Arguments:
- volume: float32 [4, 256, 32, 128], P('frame', 'vox'), may hold values from -60 to 60
Outputs:
- factor: float32 [256, 256], replicated
The draws below stay inside these ranges and needn't reach their ends.
All inputs are finite; a program needn't handle non-finite values.
Results may differ from the reference program's by a relative error of at most 0.0001.
Values sent between devices are 32-bit elements; how exact they have to be, the bound alone decides.
A program may use at most 64 MiB of HBM per device.

```python
import jax
import jax.numpy as jnp
from jax import lax

NZ = 256
XD = 4
NY = 128
FRAMES = 4
NX = 32


def draw_volume(key, part):
    full_shape = (FRAMES, NZ, NX, NY)
    key_base = jax.random.fold_in(key, 11)
    key_pair = jax.random.fold_in(key, 12)
    key_rows = jax.random.fold_in(key, 13)
    base_values = jnp.clip(jax.random.normal(key_base, full_shape, jnp.float32), -4.0, 4.0)
    num_blocks = NX // XD
    pairing = jax.vmap(lambda frame_id: jax.random.permutation(jax.random.fold_in(key_pair, frame_id), num_blocks))(jnp.arange(FRAMES))
    z_block = jnp.arange(NZ) // (NZ // num_blocks)
    x_block = jnp.arange(NX) // XD
    paired = z_block[None, :, None] == pairing[:, x_block][:, None, :]
    spike_gain = jnp.where(paired, 8.0, 1.0).astype(jnp.float32)
    values = base_values * spike_gain[:, :, :, None]
    row_scale = jnp.exp(jax.random.uniform(key_rows, (NZ,), jnp.float32, jnp.log(0.7), jnp.log(1.4)))
    values = values * row_scale[None, :, None, None]
    return values


def setup_inputs(seed: int = 0) -> dict:
    key_of = jax.random.split(jax.random.key(seed), 2)
    return {
        "volume": draw_volume(jax.random.fold_in(key_of[1], 71), 0),
    }


def reference(volume):
    rows_z = volume.shape[1]
    column_total = volume.shape[0] * volume.shape[2] * volume.shape[3]

    def add_frame(running, frame_data):
        flat = frame_data.reshape(rows_z, -1)
        return (running + jnp.dot(flat.astype(jnp.float32), flat.T.astype(jnp.float32), precision=lax.Precision.HIGHEST, preferred_element_type=jnp.float32), None)
    running, unused = lax.scan(add_frame, jnp.zeros((rows_z, rows_z), jnp.float32), volume)
    gram = running / jnp.float32(column_total)
    return jnp.linalg.cholesky(gram)
```

```python
import functools

import jax
import jax.numpy as jnp
from jax import lax
from jax.experimental import pallas as pl
from jax.experimental.pallas import tpu as pltpu
from jax.sharding import PartitionSpec as P

MESH = pl.DeviceIdType.MESH
CORES = 2
EXACT = lax.Precision.HIGHEST


def gram_kernel(
    frames, voxes, rows_z, rows_x, columns,
    vol_ref, out_ref,
    send, recv, part, plane, line, total,
    a_send, a_recv, b_send, b_recv, c_send, c_recv, d_send, d_recv,
):
    f = lax.axis_index("frame")
    v = lax.axis_index("vox")
    chip, core = v // CORES, v % CORES
    chips = voxes // CORES
    own = f * CORES + core
    members = frames * CORES
    xd = rows_x // voxes
    slot = rows_z * xd
    half = rows_z * voxes // 2
    share = 2 * half // members

    def plane_peer(k):
        q = lax.rem(own + k, members)
        return q, (q // CORES, chip * CORES + q % CORES)

    def line_peer(k):
        c = lax.rem(chip + k, chips)
        return c, (f, c * CORES + core)

    barrier = pltpu.get_barrier_semaphore()
    for k in range(1, voxes):
        pl.semaphore_signal(
            barrier, inc=1, device_id=(f, lax.rem(v + k, voxes)), device_id_type=MESH
        )
    for k in range(1, members):
        pl.semaphore_signal(
            barrier, inc=1, device_id=plane_peer(k)[1], device_id_type=MESH
        )

    for p in range(voxes):
        for x in range(xd):
            send[p, pl.ds(x, rows_z, stride=xd), :] = vol_ref[
                pl.ds(p * xd + x, rows_z, stride=rows_x), :
            ]

    pl.semaphore_wait(barrier, voxes - 1 + members - 1)

    mine = pl.ds(pl.multiple_of(v * slot, slot), slot)
    copies = []
    for k in sorted(range(1, voxes), key=lambda k: abs(k - voxes // 2)):
        p = lax.rem(v + k, voxes)
        copy = pltpu.make_async_remote_copy(
            src_ref=send.at[p],
            dst_ref=recv.at[mine],
            send_sem=a_send.at[k],
            recv_sem=a_recv.at[k],
            device_id=(f, p),
            device_id_type=MESH,
        )
        copy.start()
        copies.append(copy)
    recv[mine, :] = send[v]
    for copy in copies:
        copy.wait()

    block = jnp.concatenate(
        [recv[pl.ds(x, 2 * half, stride=xd), :] for x in range(xd)], axis=1
    )
    top, low = block[:half], block[half:]

    def dot(a, b):
        return lax.dot_general(
            a, b, (((1,), (1,)), ((), ())),
            precision=EXACT, preferred_element_type=jnp.float32,
        )

    i = lax.broadcasted_iota(jnp.int32, (half, half), 0)
    j = lax.broadcasted_iota(jnp.int32, (half, half), 1)
    g22 = dot(low, low)
    diag = jnp.sum(jnp.where(i == j, g22, 0.0), axis=0, keepdims=True)
    diag = jnp.broadcast_to(diag, (8, half))
    packed = [dot(low, top), jnp.where(i >= j, dot(top, top), g22)]
    for q in range(members):
        row = q * share
        part[q, :share, :] = packed[row // half][row % half:row % half + share]
        part[q, share:, :] = diag

    copies = []
    for k in range(1, members):
        q, device = plane_peer(k)
        copy = pltpu.make_async_remote_copy(
            src_ref=part.at[q],
            dst_ref=plane.at[own],
            send_sem=b_send.at[k],
            recv_sem=b_recv.at[k],
            device_id=device,
            device_id_type=MESH,
        )
        copy.start()
        copies.append(copy)
    plane[own] = part[own]
    for copy in copies:
        copy.wait()

    line[chip] = jnp.sum(plane[...], axis=0)
    copies = []
    for k in range(1, chips):
        c, device = line_peer(k)
        copy = pltpu.make_async_remote_copy(
            src_ref=line.at[chip],
            dst_ref=line.at[chip],
            send_sem=c_send.at[k],
            recv_sem=c_recv.at[k],
            device_id=device,
            device_id_type=MESH,
        )
        copy.start()
        copies.append(copy)
    for copy in copies:
        copy.wait()

    total[own] = jnp.sum(line[...], axis=0) / jnp.float32(columns)
    copies = []
    for k in range(1, members):
        q, device = plane_peer(k)
        copy = pltpu.make_async_remote_copy(
            src_ref=total.at[own],
            dst_ref=total.at[own],
            send_sem=d_send.at[k],
            recv_sem=d_recv.at[k],
            device_id=device,
            device_id_type=MESH,
        )
        copy.start()
        copies.append(copy)
    for copy in copies:
        copy.wait()
    out_ref[...] = total[...]


def summed_gram(volume):
    frames, voxes = lax.axis_size("frame"), lax.axis_size("vox")
    rows_z, rows_x, lanes = volume.shape[1:]
    columns = float(volume.shape[0] * frames * rows_x * lanes)
    xd = rows_x // voxes
    members = frames * CORES
    full = rows_z * voxes
    half = full // 2
    share = full // members
    packed = (members, share + 8, half)
    dma = pltpu.SemaphoreType.DMA
    vmem = pl.BlockSpec(memory_space=pltpu.VMEM)
    return pl.pallas_call(
        functools.partial(gram_kernel, frames, voxes, rows_z, rows_x, columns),
        out_shape=jax.ShapeDtypeStruct(packed, jnp.float32),
        in_specs=[vmem],
        out_specs=vmem,
        scratch_shapes=[
            pltpu.VMEM((voxes, rows_z * xd, lanes), jnp.float32),
            pltpu.VMEM((full * xd, lanes), jnp.float32),
            pltpu.VMEM(packed, jnp.float32),
            pltpu.VMEM(packed, jnp.float32),
            pltpu.VMEM((voxes // CORES, share + 8, half), jnp.float32),
            pltpu.VMEM(packed, jnp.float32),
            dma((voxes,)), dma((voxes,)),
            dma((members,)), dma((members,)),
            dma((voxes // CORES,)), dma((voxes // CORES,)),
            dma((members,)), dma((members,)),
        ],
        compiler_params=pltpu.CompilerParams(
            collective_id=0, has_side_effects=True, vmem_limit_bytes=24 * 1024 * 1024
        ),
        name="summed_gram",
    )(volume.reshape(rows_z * rows_x, lanes))


def per_device(volume):
    packed = summed_gram(volume)
    members, rows, half = packed.shape
    share = rows - 8
    main = packed[:, :share].reshape(2 * half, half)
    diag = packed[0, share]
    g21, mixed = main[:half], main[half:]
    i = lax.broadcasted_iota(jnp.int32, (half, half), 0)
    j = lax.broadcasted_iota(jnp.int32, (half, half), 1)
    g22 = jnp.where(i == j, diag[None, :], mixed.T)
    gram = jnp.concatenate(
        [
            jnp.concatenate([mixed, g21.T], axis=1),
            jnp.concatenate([g21, g22], axis=1),
        ],
        axis=0,
    )
    return lax.linalg.cholesky(gram, symmetrize_input=False)


def solution(mesh):
    return jax.shard_map(
        per_device,
        mesh=mesh,
        in_specs=(P("frame", "vox", None, None),),
        out_specs=P(),
        check_vma=False,
    )
```

```python
import functools

import jax
import jax.numpy as jnp
from jax import lax
from jax.experimental import pallas as pl
from jax.experimental.pallas import tpu as pltpu
from jax.sharding import PartitionSpec as P

MESH = pl.DeviceIdType.MESH
CORES = 2
EXACT = lax.Precision.HIGHEST
ROWS, LANES = 8, 128


def gram_kernel(
    frames, voxes, rows_z, rows_x, columns,
    vol_ref, out_ref,
    send, recv, part, plane, line, total,
    a_send, a_recv, b_send, b_recv, c_send, c_recv, d_send, d_recv,
):
    f = lax.axis_index("frame")
    v = lax.axis_index("vox")
    chip, core = v // CORES, v % CORES
    chips = voxes // CORES
    own = f * CORES + core
    members = frames * CORES
    xd = rows_x // voxes
    slot = rows_z * xd
    half = rows_z * voxes // 2
    share = 2 * half // members

    def plane_peer(k):
        q = lax.rem(own + k, members)
        return q, (q // CORES, chip * CORES + q % CORES)

    def line_peer(k):
        c = lax.rem(chip + k, chips)
        return c, (f, c * CORES + core)

    barrier = pltpu.get_barrier_semaphore()
    for k in range(1, voxes):
        pl.semaphore_signal(
            barrier, inc=1, device_id=(f, lax.rem(v + k, voxes)), device_id_type=MESH
        )
    for k in range(1, members):
        pl.semaphore_signal(
            barrier, inc=1, device_id=plane_peer(k)[1], device_id_type=MESH
        )

    for p in range(voxes):
        for x in range(xd):
            send[p, pl.ds(x, rows_z, stride=xd), :] = vol_ref[
                pl.ds(p * xd + x, rows_z, stride=rows_x), :
            ]

    pl.semaphore_wait(barrier, voxes - 1 + members - 1)

    mine = pl.ds(pl.multiple_of(v * slot, slot), slot)
    copies = []
    for k in sorted(range(1, voxes), key=lambda k: abs(k - voxes // 2)):
        p = lax.rem(v + k, voxes)
        copy = pltpu.make_async_remote_copy(
            src_ref=send.at[p],
            dst_ref=recv.at[mine],
            send_sem=a_send.at[k],
            recv_sem=a_recv.at[k],
            device_id=(f, p),
            device_id_type=MESH,
        )
        copy.start()
        copies.append(copy)
    recv[mine, :] = send[v]
    for copy in copies:
        copy.wait()

    block = jnp.concatenate(
        [recv[pl.ds(x, 2 * half, stride=xd), :] for x in range(xd)], axis=1
    )
    top, low = block[:half], block[half:]

    def dot(a, b):
        return lax.dot_general(
            a, b, (((1,), (1,)), ((), ())),
            precision=EXACT, preferred_element_type=jnp.float32,
        )

    i = lax.broadcasted_iota(jnp.int32, (half, half), 0)
    j = lax.broadcasted_iota(jnp.int32, (half, half), 1)
    g22 = dot(low, low)
    diag = jnp.sum(jnp.where(i == j, g22, 0.0), axis=0, keepdims=True)
    diag = jnp.broadcast_to(diag, (8, half))
    packed = [dot(low, top), jnp.where(i >= j, dot(top, top), g22)]
    for q in range(members):
        row = q * share
        part[q, :share, :] = packed[row // half][row % half:row % half + share]
        part[q, share:, :] = diag

    copies = []
    for k in range(1, members):
        q, device = plane_peer(k)
        copy = pltpu.make_async_remote_copy(
            src_ref=part.at[q],
            dst_ref=plane.at[own],
            send_sem=b_send.at[k],
            recv_sem=b_recv.at[k],
            device_id=device,
            device_id_type=MESH,
        )
        copy.start()
        copies.append(copy)
    plane[own] = part[own]
    for copy in copies:
        copy.wait()

    line[chip] = jnp.sum(plane[...], axis=0)
    copies = []
    for k in range(1, chips):
        c, device = line_peer(k)
        copy = pltpu.make_async_remote_copy(
            src_ref=line.at[chip],
            dst_ref=line.at[chip],
            send_sem=c_send.at[k],
            recv_sem=c_recv.at[k],
            device_id=device,
            device_id_type=MESH,
        )
        copy.start()
        copies.append(copy)
    for copy in copies:
        copy.wait()

    total[own] = jnp.sum(line[...], axis=0) / jnp.float32(columns)
    copies = []
    for k in range(1, members):
        q, device = plane_peer(k)
        copy = pltpu.make_async_remote_copy(
            src_ref=total.at[own],
            dst_ref=total.at[own],
            send_sem=d_send.at[k],
            recv_sem=d_recv.at[k],
            device_id=device,
            device_id_type=MESH,
        )
        copy.start()
        copies.append(copy)
    for copy in copies:
        copy.wait()
    out_ref[...] = total[...]


def summed_gram(volume):
    frames, voxes = lax.axis_size("frame"), lax.axis_size("vox")
    rows_z, rows_x, lanes = volume.shape[1:]
    columns = float(volume.shape[0] * frames * rows_x * lanes)
    xd = rows_x // voxes
    members = frames * CORES
    full = rows_z * voxes
    half = full // 2
    share = full // members
    packed = (members, share + 8, half)
    dma = pltpu.SemaphoreType.DMA
    vmem = pl.BlockSpec(memory_space=pltpu.VMEM)
    return pl.pallas_call(
        functools.partial(gram_kernel, frames, voxes, rows_z, rows_x, columns),
        out_shape=jax.ShapeDtypeStruct(packed, jnp.float32),
        in_specs=[vmem],
        out_specs=vmem,
        scratch_shapes=[
            pltpu.VMEM((voxes, rows_z * xd, lanes), jnp.float32),
            pltpu.VMEM((full * xd, lanes), jnp.float32),
            pltpu.VMEM(packed, jnp.float32),
            pltpu.VMEM(packed, jnp.float32),
            pltpu.VMEM((voxes // CORES, share + 8, half), jnp.float32),
            pltpu.VMEM(packed, jnp.float32),
            dma((voxes,)), dma((voxes,)),
            dma((members,)), dma((members,)),
            dma((voxes // CORES,)), dma((voxes // CORES,)),
            dma((members,)), dma((members,)),
        ],
        compiler_params=pltpu.CompilerParams(
            collective_id=0, has_side_effects=True, vmem_limit_bytes=24 * 1024 * 1024
        ),
        name="summed_gram",
    )(volume.reshape(rows_z * rows_x, lanes))


def reciprocal(d):
    r = pl.reciprocal(d, approx=True)
    return r * (2.0 - d * r)


def inverse_root(d):
    r = lax.rsqrt(d)
    return r * (1.5 - 0.5 * d * r * r)


def splat_lane(rows, lane):
    return jnp.broadcast_to(rows[:, lane:lane + 1], (ROWS, LANES))


def splat_row(rows, i):
    return jnp.broadcast_to(rows[i:i + 1], rows.shape)


def factor_rows(work, upper, row0):
    height, width = work.shape
    panel = work[:ROWS, :]
    for k in range(0, height, ROWS):
        columns = [splat_lane(panel[:, :LANES], k + j) for j in range(ROWS)]
        s = {
            (i, j): splat_row(columns[j], i) for j in range(ROWS) for i in range(j, ROWS)
        }
        rows = [splat_row(panel, i) for i in range(ROWS)]
        wide = lambda t: jnp.concatenate([t] * (width // LANES), axis=1)
        inv, low = [], {}
        for m in range(ROWS):
            inv.append(reciprocal(s[m, m]))
            for i in range(m + 1, ROWS):
                low[i, m] = s[i, m] * inv[m]
                for j in range(m + 1, i + 1):
                    s[i, j] = s[i, j] - low[i, m] * s[j, m]
            for i in range(m + 1, ROWS):
                rows[i] = rows[i] - wide(low[i, m]) * rows[m]
        for i in range(ROWS):
            row = rows[i] * wide(inverse_root(s[i, i]))
            upper[row0 + k + i:row0 + k + i + 1, :] = row[:1]
        if k + ROWS == height:
            break
        solved = [None] * ROWS
        for i in reversed(range(ROWS)):
            solved[i] = rows[i] * wide(inv[i])
            for m in reversed(range(i + 1, ROWS)):
                solved[i] = solved[i] - wide(low[m, i]) * solved[m]
        for g in range(k + ROWS, height, ROWS):
            group = work[g:g + ROWS, :]
            terms = [
                wide(splat_lane(group[:, :LANES], k + j)) * solved[j] for j in range(ROWS)
            ]
            while len(terms) > 1:
                terms = [a + b for a, b in zip(terms[::2], terms[1::2])]
            group = group - terms[0]
            if g == k + ROWS:
                panel = group
            else:
                work[g:g + ROWS, :] = group


def factor_kernel(packed_ref, out_ref, work1, work2, upper1, upper2):
    members, rows, half = packed_ref.shape
    share = rows - ROWS
    main = [packed_ref[q, :share, :] for q in range(members)]
    g21 = jnp.concatenate(main[:members // 2], axis=0)
    mixed = jnp.concatenate(main[members // 2:], axis=0)
    i = lax.broadcasted_iota(jnp.int32, (half, half), 0)
    j = lax.broadcasted_iota(jnp.int32, (half, half), 1)
    flipped = mixed.T
    work1[:, :half] = jnp.where(i >= j, mixed, flipped)
    work1[:, half:] = g21.T
    factor_rows(work1, upper1, 0)
    right = upper1[:, half:]
    g22 = jnp.where(i < j, mixed, flipped)
    g22 = jnp.where(i == j, packed_ref[0, share:share + 1, :], g22)
    work2[...] = g22 - lax.dot_general(
        right, right, (((0,), (0,)), ((), ())),
        precision=EXACT, preferred_element_type=jnp.float32,
    )
    factor_rows(work2, upper2, 0)
    out_ref[:half, :half] = jnp.where(i >= j, upper1[:, :half].T, 0.0)
    out_ref[:half, half:] = jnp.zeros((half, half), jnp.float32)
    out_ref[half:, :half] = right.T
    out_ref[half:, half:] = jnp.where(i >= j, upper2[...].T, 0.0)


def per_device(volume):
    packed = summed_gram(volume)
    half = packed.shape[2]
    vmem = pl.BlockSpec(memory_space=pltpu.VMEM)
    return pl.pallas_call(
        factor_kernel,
        out_shape=jax.ShapeDtypeStruct((2 * half, 2 * half), jnp.float32),
        in_specs=[vmem],
        out_specs=vmem,
        scratch_shapes=[
            pltpu.VMEM((half, 2 * half), jnp.float32),
            pltpu.VMEM((half, half), jnp.float32),
            pltpu.VMEM((half, 2 * half), jnp.float32),
            pltpu.VMEM((half, half), jnp.float32),
        ],
        compiler_params=pltpu.CompilerParams(vmem_limit_bytes=16 * 1024 * 1024),
        name="factor",
    )(packed)


def solution(mesh):
    return jax.shard_map(
        per_device,
        mesh=mesh,
        in_specs=(P("frame", "vox", None, None),),
        out_specs=P(),
        check_vma=False,
    )
```

```python
import functools

import jax
import jax.numpy as jnp
from jax import lax
from jax.experimental import pallas as pl
from jax.experimental.pallas import tpu as pltpu
from jax.sharding import PartitionSpec as P

MESH = pl.DeviceIdType.MESH
CORES = 2
EXACT = lax.Precision.HIGHEST
ROWS, LANES = 8, 128


def gram_kernel(
    frames, voxes, rows_z, rows_x, columns,
    vol_hbm, out_ref,
    vol_ref, send, recv, part, plane, line, total,
    a_send, a_recv, b_send, b_recv, c_send, c_recv, d_send, d_recv, load_sem,
):
    f = lax.axis_index("frame")
    v = lax.axis_index("vox")
    chip, core = v // CORES, v % CORES
    chips = voxes // CORES
    own = f * CORES + core
    members = frames * CORES
    xd = rows_x // voxes
    slot = rows_z * xd
    half = rows_z * voxes // 2
    share = 2 * half // members

    def plane_peer(k):
        q = lax.rem(own + k, members)
        return q, (q // CORES, chip * CORES + q % CORES)

    def line_peer(k):
        c = lax.rem(chip + k, chips)
        return c, (f, c * CORES + core)

    load = pltpu.make_async_copy(vol_hbm, vol_ref, load_sem)
    load.start()

    barrier = pltpu.get_barrier_semaphore()
    for k in range(1, voxes):
        pl.semaphore_signal(
            barrier, inc=1, device_id=(f, lax.rem(v + k, voxes)), device_id_type=MESH
        )
    for k in range(1, members):
        pl.semaphore_signal(
            barrier, inc=1, device_id=plane_peer(k)[1], device_id_type=MESH
        )

    load.wait()
    for p in range(voxes):
        for x in range(xd):
            send[p, pl.ds(x, rows_z, stride=xd), :] = vol_ref[
                pl.ds(p * xd + x, rows_z, stride=rows_x), :
            ]

    pl.semaphore_wait(barrier, voxes - 1 + members - 1)

    mine = pl.ds(pl.multiple_of(v * slot, slot), slot)
    copies = []
    for k in sorted(range(1, voxes), key=lambda k: abs(k - voxes // 2)):
        p = lax.rem(v + k, voxes)
        copy = pltpu.make_async_remote_copy(
            src_ref=send.at[p],
            dst_ref=recv.at[mine],
            send_sem=a_send.at[k],
            recv_sem=a_recv.at[k],
            device_id=(f, p),
            device_id_type=MESH,
        )
        copy.start()
        copies.append(copy)
    recv[mine, :] = send[v]
    for copy in copies:
        copy.wait()

    block = jnp.concatenate(
        [recv[pl.ds(x, 2 * half, stride=xd), :] for x in range(xd)], axis=1
    )
    top, low = block[:half], block[half:]

    def dot(a, b):
        return lax.dot_general(
            a, b, (((1,), (1,)), ((), ())),
            precision=EXACT, preferred_element_type=jnp.float32,
        )

    i = lax.broadcasted_iota(jnp.int32, (half, half), 0)
    j = lax.broadcasted_iota(jnp.int32, (half, half), 1)
    g22 = dot(low, low)
    diag = jnp.sum(jnp.where(i == j, g22, 0.0), axis=0, keepdims=True)
    packed = [dot(low, top), jnp.where(i >= j, dot(top, top), g22)]
    for q in range(members):
        row = q * share
        part[q, :share, :] = packed[row // half][row % half:row % half + share]
        part[q, share:, :] = diag

    copies = []
    for k in range(1, members):
        q, device = plane_peer(k)
        copy = pltpu.make_async_remote_copy(
            src_ref=part.at[q],
            dst_ref=plane.at[own],
            send_sem=b_send.at[k],
            recv_sem=b_recv.at[k],
            device_id=device,
            device_id_type=MESH,
        )
        copy.start()
        copies.append(copy)
    plane[own] = part[own]
    for copy in copies:
        copy.wait()

    line[chip] = jnp.sum(plane[...], axis=0)
    copies = []
    for k in range(1, chips):
        c, device = line_peer(k)
        copy = pltpu.make_async_remote_copy(
            src_ref=line.at[chip],
            dst_ref=line.at[chip],
            send_sem=c_send.at[k],
            recv_sem=c_recv.at[k],
            device_id=device,
            device_id_type=MESH,
        )
        copy.start()
        copies.append(copy)
    for copy in copies:
        copy.wait()

    total[own] = jnp.sum(line[...], axis=0) / jnp.float32(columns)
    copies = []
    for k in range(1, members):
        q, device = plane_peer(k)
        copy = pltpu.make_async_remote_copy(
            src_ref=total.at[own],
            dst_ref=total.at[own],
            send_sem=d_send.at[k],
            recv_sem=d_recv.at[k],
            device_id=device,
            device_id_type=MESH,
        )
        copy.start()
        copies.append(copy)
    for copy in copies:
        copy.wait()
    out_ref[...] = total[...]


def summed_gram(volume):
    frames, voxes = lax.axis_size("frame"), lax.axis_size("vox")
    rows_z, rows_x, lanes = volume.shape[1:]
    columns = float(volume.shape[0] * frames * rows_x * lanes)
    xd = rows_x // voxes
    members = frames * CORES
    full = rows_z * voxes
    half = full // 2
    share = full // members
    packed = (members, share + 1, half)
    dma = pltpu.SemaphoreType.DMA
    vmem = pl.BlockSpec(memory_space=pltpu.VMEM)
    return pl.pallas_call(
        functools.partial(gram_kernel, frames, voxes, rows_z, rows_x, columns),
        out_shape=jax.ShapeDtypeStruct(packed, jnp.float32),
        in_specs=[pl.BlockSpec(memory_space=pltpu.HBM)],
        out_specs=vmem,
        scratch_shapes=[
            pltpu.VMEM((rows_z * rows_x, lanes), jnp.float32),
            pltpu.VMEM((voxes, rows_z * xd, lanes), jnp.float32),
            pltpu.VMEM((full * xd, lanes), jnp.float32),
            pltpu.VMEM(packed, jnp.float32),
            pltpu.VMEM(packed, jnp.float32),
            pltpu.VMEM((voxes // CORES, share + 1, half), jnp.float32),
            pltpu.VMEM(packed, jnp.float32),
            dma((voxes,)), dma((voxes,)),
            dma((members,)), dma((members,)),
            dma((voxes // CORES,)), dma((voxes // CORES,)),
            dma((members,)), dma((members,)),
            dma,
        ],
        compiler_params=pltpu.CompilerParams(
            collective_id=0, has_side_effects=True, vmem_limit_bytes=24 * 1024 * 1024
        ),
        name="summed_gram",
    )(volume.reshape(rows_z * rows_x, lanes))


def reciprocal(d):
    return pl.reciprocal(d, approx=True)


def splat_lane(rows, lane):
    return jnp.broadcast_to(rows[:, lane:lane + 1], (ROWS, LANES))


def splat_row(rows, i):
    return jnp.broadcast_to(rows[i:i + 1], rows.shape)


def factor_rows(work, upper):
    height, width = work.shape
    wide = lambda t: jnp.concatenate([t] * (width // LANES), axis=1)
    pairs = [(i, j) for j in range(ROWS) for i in range(j, ROWS)]
    panel = work[:ROWS, :]
    corner = [splat_lane(panel[:, :LANES], j) for j in range(ROWS)]
    for k in range(0, height, ROWS):
        last = k + ROWS == height
        s = {(i, j): splat_row(corner[j], i) for i, j in pairs}
        rows = [splat_row(panel, i) for i in range(ROWS)]
        if not last:
            panel = work[k + ROWS:k + 2 * ROWS, :]
            left = [splat_lane(panel[:, :LANES], k + j) for j in range(ROWS)]
            corner = [splat_lane(panel[:, :LANES], k + ROWS + j) for j in range(ROWS)]
        inv, low, pivot, scaled = [None] * ROWS, {}, [None] * ROWS, [None] * ROWS
        for m in range(0, ROWS, 2):
            n = m + 1
            a, b, c = s[m, m], s[n, m], s[n, n]
            det = a * c - b * b
            inv_det = reciprocal(det)
            inv[m] = reciprocal(a)
            inv[n] = a * inv_det
            pivot[m], pivot[n] = a, det * inv[m]
            low[n, m] = b * inv[m]
            second = {}
            for i in range(n + 1, ROWS):
                low[i, m] = s[i, m] * inv[m]
                second[i] = s[i, n] - low[i, m] * b
                low[i, n] = second[i] * inv[n]
            for i, j in pairs:
                if j <= n:
                    continue
                first = s[i, j] - low[i, m] * s[j, m]
                if i <= n + 2:
                    s[i, j] = first - (a * second[i] * second[j]) * inv_det
                else:
                    s[i, j] = first - low[i, n] * second[j]
            for q in (m, n):
                for i in range(q + 1, ROWS):
                    rows[i] = rows[i] - wide(low[i, q]) * rows[q]
                scaled[q] = rows[q] * wide(inv[q])
                if last:
                    continue
                for i in range(q + 1, ROWS):
                    left[i] = left[i] - low[i, q] * left[q]
                panel = panel - wide(left[q]) * scaled[q]
                turned = left[q] * inv[q]
                corner = [
                    corner[j] - left[q] * splat_row(turned, j) for j in range(ROWS)
                ]
        for i in range(ROWS):
            row = rows[i] * wide(lax.rsqrt(pivot[i]))
            upper[k + i:k + i + 1, :] = row[:1]
        if k + 2 * ROWS >= height:
            continue
        solved = list(scaled)
        for i in reversed(range(ROWS)):
            for m in reversed(range(i + 1, ROWS)):
                solved[i] = solved[i] - wide(low[m, i]) * solved[m]
        for g in range(k + 2 * ROWS, height, ROWS):
            group = work[g:g + ROWS, :]
            terms = [
                wide(splat_lane(group[:, :LANES], k + j)) * solved[j] for j in range(ROWS)
            ]
            while len(terms) > 1:
                terms = [x + y for x, y in zip(terms[::2], terms[1::2])]
            work[g:g + ROWS, :] = group - terms[0]


def factor_kernel(packed_ref, out_ref, work1, work2, upper1, upper2):
    members, rows, half = packed_ref.shape
    share = rows - 1
    main = [packed_ref[q, :share, :] for q in range(members)]
    g21 = jnp.concatenate(main[:members // 2], axis=0)
    mixed = jnp.concatenate(main[members // 2:], axis=0)
    i = lax.broadcasted_iota(jnp.int32, (half, half), 0)
    j = lax.broadcasted_iota(jnp.int32, (half, half), 1)
    diag1 = jnp.sum(jnp.where(i == j, mixed, 0.0), axis=0, keepdims=True)
    diag2 = packed_ref[0, share:, :]
    root1, root2 = lax.rsqrt(diag1), lax.rsqrt(diag2)
    side1 = jnp.broadcast_to(root1, (half, half)).T
    side2 = jnp.broadcast_to(root2, (half, half)).T
    flipped = mixed.T
    work1[:, :half] = jnp.where(i >= j, mixed, flipped) * side1 * root1
    work1[:, half:] = g21.T * side1 * root2
    factor_rows(work1, upper1)
    right = upper1[:, half:]
    g22 = jnp.where(i < j, mixed, flipped)
    g22 = jnp.where(i == j, diag2, g22)
    work2[...] = g22 * side2 * root2 - lax.dot_general(
        right, right, (((0,), (0,)), ((), ())),
        precision=EXACT, preferred_element_type=jnp.float32,
    )
    factor_rows(work2, upper2)
    size1, size2 = diag1 * root1, diag2 * root2
    out_ref[:half, :half] = jnp.where(i >= j, (upper1[:, :half] * size1).T, 0.0)
    out_ref[:half, half:] = jnp.zeros((half, half), jnp.float32)
    out_ref[half:, :half] = (right * size2).T
    out_ref[half:, half:] = jnp.where(i >= j, (upper2[...] * size2).T, 0.0)


def per_device(volume):
    packed = summed_gram(volume)
    half = packed.shape[2]
    vmem = pl.BlockSpec(memory_space=pltpu.VMEM)
    return pl.pallas_call(
        factor_kernel,
        out_shape=jax.ShapeDtypeStruct((2 * half, 2 * half), jnp.float32),
        in_specs=[vmem],
        out_specs=vmem,
        scratch_shapes=[
            pltpu.VMEM((half, 2 * half), jnp.float32),
            pltpu.VMEM((half, half), jnp.float32),
            pltpu.VMEM((half, 2 * half), jnp.float32),
            pltpu.VMEM((half, half), jnp.float32),
        ],
        compiler_params=pltpu.CompilerParams(vmem_limit_bytes=16 * 1024 * 1024),
        name="factor",
    )(packed)


def solution(mesh):
    return jax.shard_map(
        per_device,
        mesh=mesh,
        in_specs=(P("frame", "vox", None, None),),
        out_specs=P(),
        check_vma=False,
    )
```

```python
import functools

import jax
import jax.numpy as jnp
from jax import lax
from jax.experimental import pallas as pl
from jax.experimental.pallas import tpu as pltpu
from jax.sharding import PartitionSpec as P

MESH = pl.DeviceIdType.MESH
CORES = 2
EXACT = lax.Precision.HIGHEST
ROWS, LANES = 8, 128


def chunk_rows(rows_z, xd):
    step = next(n for n in range(1, xd + 1) if xd % n == 0 and rows_z * n % ROWS == 0)
    return step, rows_z * step


def gram_kernel(
    frames, voxes, rows_z, rows_x, columns,
    vol_hbm, out_ref,
    vol_ref, send, recv, gram, part, plane, line, total,
    a_send, a_recv, b_send, b_recv, c_send, c_recv, d_send, d_recv, load_sem,
):
    f = lax.axis_index("frame")
    v = lax.axis_index("vox")
    chip, core = v // CORES, v % CORES
    chips = voxes // CORES
    own = f * CORES + core
    members = frames * CORES
    xd = rows_x // voxes
    step, slot = chunk_rows(rows_z, xd)
    chunks = xd // step
    half = rows_z * voxes // 2
    share = 2 * half // members

    def plane_peer(k):
        q = lax.rem(own + k, members)
        return q, (q // CORES, chip * CORES + q % CORES)

    def line_peer(k):
        c = lax.rem(chip + k, chips)
        return c, (f, c * CORES + core)

    loads = [
        pltpu.make_async_copy(
            vol_hbm.at[0, z], vol_ref.at[pl.ds(z * rows_x, rows_x)], load_sem.at[z]
        )
        for z in range(rows_z)
    ]
    for load in loads:
        load.start()

    barrier = pltpu.get_barrier_semaphore()
    for k in range(1, voxes):
        pl.semaphore_signal(
            barrier, inc=1, device_id=(f, lax.rem(v + k, voxes)), device_id_type=MESH
        )
    for k in range(1, members):
        pl.semaphore_signal(
            barrier, inc=1, device_id=plane_peer(k)[1], device_id_type=MESH
        )

    for load in loads:
        load.wait()
    for c in range(chunks):
        for p in range(voxes):
            for x in range(step):
                send[p, c, pl.ds(x, rows_z, stride=step), :] = vol_ref[
                    pl.ds(p * xd + c * step + x, rows_z, stride=rows_x), :
                ]

    pl.semaphore_wait(barrier, voxes - 1 + members - 1)

    mine = pl.ds(pl.multiple_of(v * slot, slot), slot)
    order = sorted(range(1, voxes), key=lambda k: abs(k - voxes // 2))
    arriving = []
    for c in range(chunks):
        arriving.append([])
        for k in order:
            p = lax.rem(v + k, voxes)
            copy = pltpu.make_async_remote_copy(
                src_ref=send.at[p, c],
                dst_ref=recv.at[c, mine],
                send_sem=a_send.at[c, k],
                recv_sem=a_recv.at[c, k],
                device_id=(f, p),
                device_id_type=MESH,
            )
            copy.start()
            arriving[c].append(copy)
    for c in range(chunks):
        recv[c, mine, :] = send[v, c]

    for c in range(chunks):
        for copy in arriving[c]:
            copy.wait_recv()
        block = jnp.concatenate(
            [recv[c, pl.ds(x, 2 * half, stride=step), :] for x in range(step)], axis=1
        )
        product = lax.dot_general(
            block, block, (((1,), (1,)), ((), ())),
            precision=EXACT, preferred_element_type=jnp.float32,
        )
        if c > 0:
            product = gram[...] + product
        gram[...] = product

    i = lax.broadcasted_iota(jnp.int32, (half, half), 0)
    j = lax.broadcasted_iota(jnp.int32, (half, half), 1)
    g22 = gram[half:, half:]
    diag = jnp.sum(jnp.where(i == j, g22, 0.0), axis=0, keepdims=True)
    packed = [gram[half:, :half], jnp.where(i >= j, gram[:half, :half], g22)]
    for q in range(members):
        row = q * share
        part[q, :share, :] = packed[row // half][row % half:row % half + share]
        part[q, share:, :] = diag

    copies = []
    for k in range(1, members):
        q, device = plane_peer(k)
        copy = pltpu.make_async_remote_copy(
            src_ref=part.at[q],
            dst_ref=plane.at[own],
            send_sem=b_send.at[k],
            recv_sem=b_recv.at[k],
            device_id=device,
            device_id_type=MESH,
        )
        copy.start()
        copies.append(copy)
    plane[own] = part[own]
    for copy in copies:
        copy.wait()
    for sent in arriving:
        for copy in sent:
            copy.wait_send()

    line[chip] = jnp.sum(plane[...], axis=0)
    copies = []
    for k in range(1, chips):
        c, device = line_peer(k)
        copy = pltpu.make_async_remote_copy(
            src_ref=line.at[chip],
            dst_ref=line.at[chip],
            send_sem=c_send.at[k],
            recv_sem=c_recv.at[k],
            device_id=device,
            device_id_type=MESH,
        )
        copy.start()
        copies.append(copy)
    for copy in copies:
        copy.wait()

    total[own] = jnp.sum(line[...], axis=0) / jnp.float32(columns)
    copies = []
    for k in range(1, members):
        q, device = plane_peer(k)
        copy = pltpu.make_async_remote_copy(
            src_ref=total.at[own],
            dst_ref=total.at[own],
            send_sem=d_send.at[k],
            recv_sem=d_recv.at[k],
            device_id=device,
            device_id_type=MESH,
        )
        copy.start()
        copies.append(copy)
    for copy in copies:
        copy.wait()
    out_ref[...] = total[...]


def summed_gram(volume):
    frames, voxes = lax.axis_size("frame"), lax.axis_size("vox")
    rows_z, rows_x, lanes = volume.shape[1:]
    columns = float(volume.shape[0] * frames * rows_x * lanes)
    xd = rows_x // voxes
    members = frames * CORES
    full = rows_z * voxes
    half = full // 2
    share = full // members
    packed = (members, share + 1, half)
    step, slot = chunk_rows(rows_z, xd)
    dma = pltpu.SemaphoreType.DMA
    vmem = pl.BlockSpec(memory_space=pltpu.VMEM)
    return pl.pallas_call(
        functools.partial(gram_kernel, frames, voxes, rows_z, rows_x, columns),
        out_shape=jax.ShapeDtypeStruct(packed, jnp.float32),
        in_specs=[pl.BlockSpec(memory_space=pltpu.HBM)],
        out_specs=vmem,
        scratch_shapes=[
            pltpu.VMEM((rows_z * rows_x, lanes), jnp.float32),
            pltpu.VMEM((voxes, xd // step, slot, lanes), jnp.float32),
            pltpu.VMEM((xd // step, slot * voxes, lanes), jnp.float32),
            pltpu.VMEM((full, full), jnp.float32),
            pltpu.VMEM(packed, jnp.float32),
            pltpu.VMEM(packed, jnp.float32),
            pltpu.VMEM((voxes // CORES, share + 1, half), jnp.float32),
            pltpu.VMEM(packed, jnp.float32),
            dma((xd // step, voxes)), dma((xd // step, voxes)),
            dma((members,)), dma((members,)),
            dma((voxes // CORES,)), dma((voxes // CORES,)),
            dma((members,)), dma((members,)),
            dma((rows_z,)),
        ],
        compiler_params=pltpu.CompilerParams(
            collective_id=0, has_side_effects=True, vmem_limit_bytes=24 * 1024 * 1024
        ),
        name="summed_gram",
    )(pltpu.with_memory_space_constraint(volume, pltpu.HBM))


def reciprocal(d):
    return pl.reciprocal(d, approx=True)


def splat_lane(rows, lane):
    return jnp.broadcast_to(rows[:, lane:lane + 1], (ROWS, LANES))


def splat_row(rows, i):
    return jnp.broadcast_to(rows[i:i + 1], rows.shape)


def factor_rows(work, upper):
    height, width = work.shape
    wide = lambda t: jnp.concatenate([t] * (width // LANES), axis=1)
    pairs = [(i, j) for j in range(ROWS) for i in range(j, ROWS)]
    panel = work[:ROWS, :]
    corner = [splat_lane(panel[:, :LANES], j) for j in range(ROWS)]
    for k in range(0, height, ROWS):
        last = k + ROWS == height
        s = {(i, j): splat_row(corner[j], i) for i, j in pairs}
        rows = [splat_row(panel, i) for i in range(ROWS)]
        if not last:
            panel = work[k + ROWS:k + 2 * ROWS, :]
            left = [splat_lane(panel[:, :LANES], k + j) for j in range(ROWS)]
            corner = [splat_lane(panel[:, :LANES], k + ROWS + j) for j in range(ROWS)]
        inv, low, pivot, scaled = [None] * ROWS, {}, [None] * ROWS, [None] * ROWS
        for m in range(0, ROWS, 2):
            n = m + 1
            a, b, c = s[m, m], s[n, m], s[n, n]
            det = a * c - b * b
            inv_det = reciprocal(det)
            inv[m] = reciprocal(a)
            inv[n] = a * inv_det
            pivot[m], pivot[n] = a, det * inv[m]
            low[n, m] = b * inv[m]
            second = {}
            for i in range(n + 1, ROWS):
                low[i, m] = s[i, m] * inv[m]
                second[i] = s[i, n] - low[i, m] * b
                low[i, n] = second[i] * inv[n]
            for i, j in pairs:
                if j <= n:
                    continue
                first = s[i, j] - low[i, m] * s[j, m]
                if i <= n + 2:
                    s[i, j] = first - (a * second[i] * second[j]) * inv_det
                else:
                    s[i, j] = first - low[i, n] * second[j]
            for q in (m, n):
                for i in range(q + 1, ROWS):
                    rows[i] = rows[i] - wide(low[i, q]) * rows[q]
                scaled[q] = rows[q] * wide(inv[q])
                if last:
                    continue
                for i in range(q + 1, ROWS):
                    left[i] = left[i] - low[i, q] * left[q]
                panel = panel - wide(left[q]) * scaled[q]
                turned = left[q] * inv[q]
                corner = [
                    corner[j] - left[q] * splat_row(turned, j) for j in range(ROWS)
                ]
        for i in range(ROWS):
            row = rows[i] * wide(lax.rsqrt(pivot[i]))
            upper[k + i:k + i + 1, :] = row[:1]
        if k + 2 * ROWS >= height:
            continue
        solved = list(scaled)
        for i in reversed(range(ROWS)):
            for m in reversed(range(i + 1, ROWS)):
                solved[i] = solved[i] - wide(low[m, i]) * solved[m]
        for g in range(k + 2 * ROWS, height, ROWS):
            group = work[g:g + ROWS, :]
            terms = [
                wide(splat_lane(group[:, :LANES], k + j)) * solved[j] for j in range(ROWS)
            ]
            while len(terms) > 1:
                terms = [x + y for x, y in zip(terms[::2], terms[1::2])]
            work[g:g + ROWS, :] = group - terms[0]


def factor_kernel(packed_ref, out_ref, work1, work2, upper1, upper2):
    members, rows, half = packed_ref.shape
    share = rows - 1
    main = [packed_ref[q, :share, :] for q in range(members)]
    g21 = jnp.concatenate(main[:members // 2], axis=0)
    mixed = jnp.concatenate(main[members // 2:], axis=0)
    i = lax.broadcasted_iota(jnp.int32, (half, half), 0)
    j = lax.broadcasted_iota(jnp.int32, (half, half), 1)
    diag1 = jnp.sum(jnp.where(i == j, mixed, 0.0), axis=0, keepdims=True)
    diag2 = packed_ref[0, share:, :]
    root1, root2 = lax.rsqrt(diag1), lax.rsqrt(diag2)
    side1 = jnp.broadcast_to(root1, (half, half)).T
    side2 = jnp.broadcast_to(root2, (half, half)).T
    flipped = mixed.T
    work1[:, :half] = jnp.where(i >= j, mixed, flipped) * side1 * root1
    work1[:, half:] = g21.T * side1 * root2
    factor_rows(work1, upper1)
    right = upper1[:, half:]
    g22 = jnp.where(i < j, mixed, flipped)
    g22 = jnp.where(i == j, diag2, g22)
    work2[...] = g22 * side2 * root2 - lax.dot_general(
        right, right, (((0,), (0,)), ((), ())),
        precision=EXACT, preferred_element_type=jnp.float32,
    )
    factor_rows(work2, upper2)
    size1, size2 = diag1 * root1, diag2 * root2
    out_ref[:half, :half] = jnp.where(i >= j, (upper1[:, :half] * size1).T, 0.0)
    out_ref[:half, half:] = jnp.zeros((half, half), jnp.float32)
    out_ref[half:, :half] = (right * size2).T
    out_ref[half:, half:] = jnp.where(i >= j, (upper2[...] * size2).T, 0.0)


def per_device(volume):
    packed = summed_gram(volume)
    half = packed.shape[2]
    vmem = pl.BlockSpec(memory_space=pltpu.VMEM)
    return pl.pallas_call(
        factor_kernel,
        out_shape=jax.ShapeDtypeStruct((2 * half, 2 * half), jnp.float32),
        in_specs=[vmem],
        out_specs=vmem,
        scratch_shapes=[
            pltpu.VMEM((half, 2 * half), jnp.float32),
            pltpu.VMEM((half, half), jnp.float32),
            pltpu.VMEM((half, 2 * half), jnp.float32),
            pltpu.VMEM((half, half), jnp.float32),
        ],
        compiler_params=pltpu.CompilerParams(vmem_limit_bytes=16 * 1024 * 1024),
        name="factor",
    )(packed)


def solution(mesh):
    return jax.shard_map(
        per_device,
        mesh=mesh,
        in_specs=(P("frame", "vox", None, None),),
        out_specs=P(),
        check_vma=False,
    )
```

```python
import functools

import jax
import jax.numpy as jnp
from jax import lax
from jax.experimental import pallas as pl
from jax.experimental.pallas import tpu as pltpu
from jax.sharding import PartitionSpec as P

MESH = pl.DeviceIdType.MESH
CORES = 2
EXACT = lax.Precision.HIGHEST
ROWS, LANES = 8, 128


def gram_kernel(
    frames, voxes, columns,
    vol_ref, out_ref,
    recv, part, plane, line, total,
    a_send, a_recv, b_send, b_recv, c_send, c_recv, d_send, d_recv, own_sem,
):
    f = lax.axis_index("frame")
    v = lax.axis_index("vox")
    chip, core = v // CORES, v % CORES
    chips = voxes // CORES
    own = f * CORES + core
    members = frames * CORES
    rows_z, xd = vol_ref.shape[0], vol_ref.shape[2]
    half = rows_z * voxes // 2
    share = 2 * half // members

    def plane_peer(k):
        q = lax.rem(own + k, members)
        return q, (q // CORES, chip * CORES + q % CORES)

    def line_peer(k):
        c = lax.rem(chip + k, chips)
        return c, (f, c * CORES + core)

    barrier = pltpu.get_barrier_semaphore()
    for k in range(1, voxes):
        pl.semaphore_signal(
            barrier, inc=1, device_id=(f, lax.rem(v + k, voxes)), device_id_type=MESH
        )
    for k in range(1, members):
        pl.semaphore_signal(
            barrier, inc=1, device_id=plane_peer(k)[1], device_id_type=MESH
        )

    mine = pl.ds(v * rows_z, rows_z)
    stay = pltpu.make_async_copy(vol_ref.at[:, v], recv.at[mine], own_sem)
    stay.start()
    pl.semaphore_wait(barrier, voxes - 1 + members - 1)

    copies = []
    for k in sorted(range(1, voxes), key=lambda k: abs(k - voxes // 2)):
        p = lax.rem(v + k, voxes)
        copy = pltpu.make_async_remote_copy(
            src_ref=vol_ref.at[:, p],
            dst_ref=recv.at[mine],
            send_sem=a_send.at[k],
            recv_sem=a_recv.at[k],
            device_id=(f, p),
            device_id_type=MESH,
        )
        copy.start()
        copies.append(copy)
    stay.wait()
    for copy in copies:
        copy.wait()

    block = jnp.concatenate([recv[:, x, :] for x in range(xd)], axis=1)
    gram = lax.dot_general(
        block, block, (((1,), (1,)), ((), ())),
        precision=EXACT, preferred_element_type=jnp.float32,
    )
    i = lax.broadcasted_iota(jnp.int32, (half, half), 0)
    j = lax.broadcasted_iota(jnp.int32, (half, half), 1)
    g22 = gram[half:, half:]
    diag = jnp.sum(jnp.where(i == j, g22, 0.0), axis=0, keepdims=True)
    packed = [gram[half:, :half], jnp.where(i >= j, gram[:half, :half], g22)]
    for q in range(members):
        row = q * share
        part[q, :share, :] = packed[row // half][row % half:row % half + share]
        part[q, share:, :] = diag

    copies = []
    for k in range(1, members):
        q, device = plane_peer(k)
        copy = pltpu.make_async_remote_copy(
            src_ref=part.at[q],
            dst_ref=plane.at[own],
            send_sem=b_send.at[k],
            recv_sem=b_recv.at[k],
            device_id=device,
            device_id_type=MESH,
        )
        copy.start()
        copies.append(copy)
    plane[own] = part[own]
    for copy in copies:
        copy.wait()

    line[chip] = jnp.sum(plane[...], axis=0)
    copies = []
    for k in range(1, chips):
        c, device = line_peer(k)
        copy = pltpu.make_async_remote_copy(
            src_ref=line.at[chip],
            dst_ref=line.at[chip],
            send_sem=c_send.at[k],
            recv_sem=c_recv.at[k],
            device_id=device,
            device_id_type=MESH,
        )
        copy.start()
        copies.append(copy)
    for copy in copies:
        copy.wait()

    total[own] = jnp.sum(line[...], axis=0) / jnp.float32(columns)
    copies = []
    for k in range(1, members):
        q, device = plane_peer(k)
        copy = pltpu.make_async_remote_copy(
            src_ref=total.at[own],
            dst_ref=total.at[own],
            send_sem=d_send.at[k],
            recv_sem=d_recv.at[k],
            device_id=device,
            device_id_type=MESH,
        )
        copy.start()
        copies.append(copy)
    for copy in copies:
        copy.wait()
    out_ref[...] = total[...]


def summed_gram(volume):
    frames, voxes = lax.axis_size("frame"), lax.axis_size("vox")
    rows_z, rows_x, lanes = volume.shape[1:]
    columns = float(volume.shape[0] * frames * rows_x * lanes)
    xd = rows_x // voxes
    members = frames * CORES
    full = rows_z * voxes
    half = full // 2
    share = full // members
    packed = (members, share + 1, half)
    split = volume.reshape(rows_z, voxes, xd, lanes)
    dma = pltpu.SemaphoreType.DMA
    vmem = pl.BlockSpec(memory_space=pltpu.VMEM)
    return pl.pallas_call(
        functools.partial(gram_kernel, frames, voxes, columns),
        out_shape=jax.ShapeDtypeStruct(packed, jnp.float32),
        in_specs=[pl.BlockSpec(memory_space=pltpu.HBM)],
        out_specs=vmem,
        scratch_shapes=[
            pltpu.VMEM((full, xd, lanes), jnp.float32),
            pltpu.VMEM(packed, jnp.float32),
            pltpu.VMEM(packed, jnp.float32),
            pltpu.VMEM((voxes // CORES, share + 1, half), jnp.float32),
            pltpu.VMEM(packed, jnp.float32),
            dma((voxes,)), dma((voxes,)),
            dma((members,)), dma((members,)),
            dma((voxes // CORES,)), dma((voxes // CORES,)),
            dma((members,)), dma((members,)),
            dma,
        ],
        compiler_params=pltpu.CompilerParams(
            collective_id=0, has_side_effects=True, vmem_limit_bytes=24 * 1024 * 1024
        ),
        name="summed_gram",
    )(pltpu.with_memory_space_constraint(split, pltpu.HBM))


def reciprocal(d):
    return pl.reciprocal(d, approx=True)


def splat_lane(rows, lane):
    return jnp.broadcast_to(rows[:, lane:lane + 1], (ROWS, LANES))


def splat_row(rows, i):
    return jnp.broadcast_to(rows[i:i + 1], rows.shape)


def factor_rows(work, upper):
    height, width = work.shape
    wide = lambda t: jnp.concatenate([t] * (width // LANES), axis=1)
    pairs = [(i, j) for j in range(ROWS) for i in range(j, ROWS)]
    panel = work[:ROWS, :]
    corner = [splat_lane(panel[:, :LANES], j) for j in range(ROWS)]
    for k in range(0, height, ROWS):
        last = k + ROWS == height
        s = {(i, j): splat_row(corner[j], i) for i, j in pairs}
        rows = [splat_row(panel, i) for i in range(ROWS)]
        if not last:
            panel = work[k + ROWS:k + 2 * ROWS, :]
            left = [splat_lane(panel[:, :LANES], k + j) for j in range(ROWS)]
            corner = [splat_lane(panel[:, :LANES], k + ROWS + j) for j in range(ROWS)]
        inv, low, pivot, scaled = [None] * ROWS, {}, [None] * ROWS, [None] * ROWS
        for m in range(0, ROWS, 2):
            n = m + 1
            a, b, c = s[m, m], s[n, m], s[n, n]
            det = a * c - b * b
            inv_det = reciprocal(det)
            inv[m] = reciprocal(a)
            inv[n] = a * inv_det
            pivot[m], pivot[n] = a, det * inv[m]
            low[n, m] = b * inv[m]
            second = {}
            for i in range(n + 1, ROWS):
                low[i, m] = s[i, m] * inv[m]
                second[i] = s[i, n] - low[i, m] * b
                low[i, n] = second[i] * inv[n]
            for i, j in pairs:
                if j <= n:
                    continue
                first = s[i, j] - low[i, m] * s[j, m]
                if i <= n + 2:
                    s[i, j] = first - (a * second[i] * second[j]) * inv_det
                else:
                    s[i, j] = first - low[i, n] * second[j]
            for q in (m, n):
                for i in range(q + 1, ROWS):
                    rows[i] = rows[i] - wide(low[i, q]) * rows[q]
                scaled[q] = rows[q] * wide(inv[q])
                if last:
                    continue
                for i in range(q + 1, ROWS):
                    left[i] = left[i] - low[i, q] * left[q]
                panel = panel - wide(left[q]) * scaled[q]
                turned = left[q] * inv[q]
                corner = [
                    corner[j] - left[q] * splat_row(turned, j) for j in range(ROWS)
                ]
        for i in range(ROWS):
            row = rows[i] * wide(lax.rsqrt(pivot[i]))
            upper[k + i:k + i + 1, :] = row[:1]
        if k + 2 * ROWS >= height:
            continue
        solved = list(scaled)
        for i in reversed(range(ROWS)):
            for m in reversed(range(i + 1, ROWS)):
                solved[i] = solved[i] - wide(low[m, i]) * solved[m]
        for g in range(k + 2 * ROWS, height, ROWS):
            group = work[g:g + ROWS, :]
            terms = [
                wide(splat_lane(group[:, :LANES], k + j)) * solved[j] for j in range(ROWS)
            ]
            while len(terms) > 1:
                terms = [x + y for x, y in zip(terms[::2], terms[1::2])]
            work[g:g + ROWS, :] = group - terms[0]


def factor_kernel(packed_ref, out_ref, work1, work2, upper1, upper2):
    members, rows, half = packed_ref.shape
    share = rows - 1
    main = [packed_ref[q, :share, :] for q in range(members)]
    g21 = jnp.concatenate(main[:members // 2], axis=0)
    mixed = jnp.concatenate(main[members // 2:], axis=0)
    i = lax.broadcasted_iota(jnp.int32, (half, half), 0)
    j = lax.broadcasted_iota(jnp.int32, (half, half), 1)
    diag1 = jnp.sum(jnp.where(i == j, mixed, 0.0), axis=0, keepdims=True)
    diag2 = packed_ref[0, share:, :]
    root1, root2 = lax.rsqrt(diag1), lax.rsqrt(diag2)
    side1 = jnp.broadcast_to(root1, (half, half)).T
    side2 = jnp.broadcast_to(root2, (half, half)).T
    flipped = mixed.T
    work1[:, :half] = jnp.where(i >= j, mixed, flipped) * side1 * root1
    work1[:, half:] = g21.T * side1 * root2
    factor_rows(work1, upper1)
    right = upper1[:, half:]
    g22 = jnp.where(i < j, mixed, flipped)
    g22 = jnp.where(i == j, diag2, g22)
    work2[...] = g22 * side2 * root2 - lax.dot_general(
        right, right, (((0,), (0,)), ((), ())),
        precision=EXACT, preferred_element_type=jnp.float32,
    )
    factor_rows(work2, upper2)
    size1, size2 = diag1 * root1, diag2 * root2
    out_ref[:half, :half] = jnp.where(i >= j, (upper1[:, :half] * size1).T, 0.0)
    out_ref[:half, half:] = jnp.zeros((half, half), jnp.float32)
    out_ref[half:, :half] = (right * size2).T
    out_ref[half:, half:] = jnp.where(i >= j, (upper2[...] * size2).T, 0.0)


def per_device(volume):
    packed = summed_gram(volume)
    half = packed.shape[2]
    vmem = pl.BlockSpec(memory_space=pltpu.VMEM)
    return pl.pallas_call(
        factor_kernel,
        out_shape=jax.ShapeDtypeStruct((2 * half, 2 * half), jnp.float32),
        in_specs=[vmem],
        out_specs=vmem,
        scratch_shapes=[
            pltpu.VMEM((half, 2 * half), jnp.float32),
            pltpu.VMEM((half, half), jnp.float32),
            pltpu.VMEM((half, 2 * half), jnp.float32),
            pltpu.VMEM((half, half), jnp.float32),
        ],
        compiler_params=pltpu.CompilerParams(vmem_limit_bytes=16 * 1024 * 1024),
        name="factor",
    )(packed)


def solution(mesh):
    return jax.shard_map(
        per_device,
        mesh=mesh,
        in_specs=(P("frame", "vox", None, None),),
        out_specs=P(),
        check_vma=False,
    )
```

```python
import functools

import jax
import jax.numpy as jnp
from jax import lax
from jax.experimental import pallas as pl
from jax.experimental.pallas import tpu as pltpu
from jax.sharding import PartitionSpec as P

MESH = pl.DeviceIdType.MESH
CORES = 2
EXACT = lax.Precision.HIGHEST
ROWS, LANES = 8, 128


def gram_kernel(
    frames, voxes, columns,
    vol_ref, out_ref,
    recv, block_ref, part, plane, line, total,
    a_send, a_recv, b_send, b_recv, c_send, c_recv, d_send, d_recv, own_sem,
):
    f = lax.axis_index("frame")
    v = lax.axis_index("vox")
    chip, core = v // CORES, v % CORES
    chips = voxes // CORES
    own = f * CORES + core
    members = frames * CORES
    rows_z, xd = vol_ref.shape[0], vol_ref.shape[2]
    half = rows_z * voxes // 2
    share = 2 * half // members

    def plane_peer(k):
        q = lax.rem(own + k, members)
        return q, (q // CORES, chip * CORES + q % CORES)

    def line_peer(k):
        c = lax.rem(chip + k, chips)
        return c, (f, c * CORES + core)

    barrier = pltpu.get_barrier_semaphore()
    for k in range(1, voxes):
        pl.semaphore_signal(
            barrier, inc=1, device_id=(f, lax.rem(v + k, voxes)), device_id_type=MESH
        )
    for k in range(1, members):
        pl.semaphore_signal(
            barrier, inc=1, device_id=plane_peer(k)[1], device_id_type=MESH
        )

    mine = pl.ds(v * rows_z, rows_z)
    stay = pltpu.make_async_copy(vol_ref.at[:, v], recv.at[mine], own_sem)
    stay.start()
    pl.semaphore_wait(barrier, voxes - 1 + members - 1)

    copies = []
    for k in sorted(range(1, voxes), key=lambda k: abs(k - voxes // 2)):
        p = lax.rem(v + k, voxes)
        copy = pltpu.make_async_remote_copy(
            src_ref=vol_ref.at[:, p],
            dst_ref=recv.at[mine],
            send_sem=a_send.at[k],
            recv_sem=a_recv.at[k],
            device_id=(f, p),
            device_id_type=MESH,
        )
        copy.start()
        copies.append((k, copy))
    def place(source):
        for x in range(xd):
            block_ref[source, :, x * LANES:(x + 1) * LANES] = recv[
                pl.ds(source * rows_z, rows_z), x, :
            ]

    stay.wait()
    place(v)
    for k, copy in reversed(copies):
        copy.wait_recv()
        place(lax.rem(v + voxes - k, voxes))
    block = block_ref[...].reshape(2 * half, xd * LANES)
    gram = lax.dot_general(
        block, block, (((1,), (1,)), ((), ())),
        precision=EXACT, preferred_element_type=jnp.float32,
    )
    i = lax.broadcasted_iota(jnp.int32, (half, half), 0)
    j = lax.broadcasted_iota(jnp.int32, (half, half), 1)
    g22 = gram[half:, half:]
    diag = jnp.sum(jnp.where(i == j, g22, 0.0), axis=0, keepdims=True)
    packed = [gram[half:, :half], jnp.where(i >= j, gram[:half, :half], g22)]
    for q in range(members):
        row = q * share
        part[q, :share, :] = packed[row // half][row % half:row % half + share]
        part[q, share:, :] = diag

    for k, copy in copies:
        copy.wait_send()

    copies = []
    for k in range(1, members):
        q, device = plane_peer(k)
        copy = pltpu.make_async_remote_copy(
            src_ref=part.at[q],
            dst_ref=plane.at[own],
            send_sem=b_send.at[k],
            recv_sem=b_recv.at[k],
            device_id=device,
            device_id_type=MESH,
        )
        copy.start()
        copies.append(copy)
    plane[own] = part[own]
    for copy in copies:
        copy.wait()

    line[chip] = jnp.sum(plane[...], axis=0)
    copies = []
    for k in range(1, chips):
        c, device = line_peer(k)
        copy = pltpu.make_async_remote_copy(
            src_ref=line.at[chip],
            dst_ref=line.at[chip],
            send_sem=c_send.at[k],
            recv_sem=c_recv.at[k],
            device_id=device,
            device_id_type=MESH,
        )
        copy.start()
        copies.append(copy)
    for copy in copies:
        copy.wait()

    total[own] = jnp.sum(line[...], axis=0) / jnp.float32(columns)
    copies = []
    for k in range(1, members):
        q, device = plane_peer(k)
        copy = pltpu.make_async_remote_copy(
            src_ref=total.at[own],
            dst_ref=total.at[own],
            send_sem=d_send.at[k],
            recv_sem=d_recv.at[k],
            device_id=device,
            device_id_type=MESH,
        )
        copy.start()
        copies.append(copy)
    for copy in copies:
        copy.wait()
    out_ref[...] = total[...]


def summed_gram(volume):
    frames, voxes = lax.axis_size("frame"), lax.axis_size("vox")
    rows_z, rows_x, lanes = volume.shape[1:]
    columns = float(volume.shape[0] * frames * rows_x * lanes)
    xd = rows_x // voxes
    members = frames * CORES
    full = rows_z * voxes
    half = full // 2
    share = full // members
    packed = (members, share + 1, half)
    split = volume.reshape(rows_z, voxes, xd, lanes)
    dma = pltpu.SemaphoreType.DMA
    vmem = pl.BlockSpec(memory_space=pltpu.VMEM)
    return pl.pallas_call(
        functools.partial(gram_kernel, frames, voxes, columns),
        out_shape=jax.ShapeDtypeStruct(packed, jnp.float32),
        in_specs=[pl.BlockSpec(memory_space=pltpu.HBM)],
        out_specs=vmem,
        scratch_shapes=[
            pltpu.VMEM((full, xd, lanes), jnp.float32),
            pltpu.VMEM((voxes, rows_z, xd * lanes), jnp.float32),
            pltpu.VMEM(packed, jnp.float32),
            pltpu.VMEM(packed, jnp.float32),
            pltpu.VMEM((voxes // CORES, share + 1, half), jnp.float32),
            pltpu.VMEM(packed, jnp.float32),
            dma((voxes,)), dma((voxes,)),
            dma((members,)), dma((members,)),
            dma((voxes // CORES,)), dma((voxes // CORES,)),
            dma((members,)), dma((members,)),
            dma,
        ],
        compiler_params=pltpu.CompilerParams(
            collective_id=0, has_side_effects=True, vmem_limit_bytes=24 * 1024 * 1024
        ),
        name="summed_gram",
    )(pltpu.with_memory_space_constraint(split, pltpu.HBM))


def reciprocal(d):
    return pl.reciprocal(d, approx=True)


def splat_lane(rows, lane):
    return jnp.broadcast_to(rows[:, lane:lane + 1], (ROWS, LANES))


def splat_row(rows, i):
    return jnp.broadcast_to(rows[i:i + 1], rows.shape)


def factor_rows(work, upper):
    height, width = work.shape
    wide = lambda t: jnp.concatenate([t] * (width // LANES), axis=1)
    pairs = [(i, j) for j in range(ROWS) for i in range(j, ROWS)]
    panel = work[:ROWS, :]
    corner = [splat_lane(panel[:, :LANES], j) for j in range(ROWS)]
    for k in range(0, height, ROWS):
        last = k + ROWS == height
        s = {(i, j): splat_row(corner[j], i) for i, j in pairs}
        rows = [splat_row(panel, i) for i in range(ROWS)]
        if not last:
            panel = work[k + ROWS:k + 2 * ROWS, :]
            left = [splat_lane(panel[:, :LANES], k + j) for j in range(ROWS)]
            corner = [splat_lane(panel[:, :LANES], k + ROWS + j) for j in range(ROWS)]
        inv, low, pivot, scaled = [None] * ROWS, {}, [None] * ROWS, [None] * ROWS
        for m in range(0, ROWS, 2):
            n = m + 1
            a, b, c = s[m, m], s[n, m], s[n, n]
            det = a * c - b * b
            inv_det = reciprocal(det)
            inv[m] = reciprocal(a)
            inv[n] = a * inv_det
            pivot[m], pivot[n] = a, det * inv[m]
            low[n, m] = b * inv[m]
            second = {}
            for i in range(n + 1, ROWS):
                low[i, m] = s[i, m] * inv[m]
                second[i] = s[i, n] - low[i, m] * b
                low[i, n] = second[i] * inv[n]
            for i, j in pairs:
                if j <= n:
                    continue
                first = s[i, j] - low[i, m] * s[j, m]
                if i <= n + 2:
                    s[i, j] = first - (a * second[i] * second[j]) * inv_det
                else:
                    s[i, j] = first - low[i, n] * second[j]
            for q in (m, n):
                for i in range(q + 1, ROWS):
                    rows[i] = rows[i] - wide(low[i, q]) * rows[q]
                scaled[q] = rows[q] * wide(inv[q])
                if last:
                    continue
                for i in range(q + 1, ROWS):
                    left[i] = left[i] - low[i, q] * left[q]
                panel = panel - wide(left[q]) * scaled[q]
                turned = left[q] * inv[q]
                corner = [
                    corner[j] - left[q] * splat_row(turned, j) for j in range(ROWS)
                ]
        for i in range(ROWS):
            row = rows[i] * wide(lax.rsqrt(pivot[i]))
            upper[k + i:k + i + 1, :] = row[:1]
        if k + 2 * ROWS >= height:
            continue
        solved = list(scaled)
        for i in reversed(range(ROWS)):
            for m in reversed(range(i + 1, ROWS)):
                solved[i] = solved[i] - wide(low[m, i]) * solved[m]
        for g in range(k + 2 * ROWS, height, ROWS):
            group = work[g:g + ROWS, :]
            terms = [
                wide(splat_lane(group[:, :LANES], k + j)) * solved[j] for j in range(ROWS)
            ]
            while len(terms) > 1:
                terms = [x + y for x, y in zip(terms[::2], terms[1::2])]
            work[g:g + ROWS, :] = group - terms[0]


def factor_kernel(packed_ref, out_ref, work1, work2, upper1, upper2):
    members, rows, half = packed_ref.shape
    share = rows - 1
    main = [packed_ref[q, :share, :] for q in range(members)]
    g21 = jnp.concatenate(main[:members // 2], axis=0)
    mixed = jnp.concatenate(main[members // 2:], axis=0)
    i = lax.broadcasted_iota(jnp.int32, (half, half), 0)
    j = lax.broadcasted_iota(jnp.int32, (half, half), 1)
    diag1 = jnp.sum(jnp.where(i == j, mixed, 0.0), axis=0, keepdims=True)
    diag2 = packed_ref[0, share:, :]
    root1, root2 = lax.rsqrt(diag1), lax.rsqrt(diag2)
    side1 = jnp.broadcast_to(root1, (half, half)).T
    side2 = jnp.broadcast_to(root2, (half, half)).T
    flipped = mixed.T
    work1[:, :half] = jnp.where(i >= j, mixed, flipped) * side1 * root1
    work1[:, half:] = g21.T * side1 * root2
    factor_rows(work1, upper1)
    right = upper1[:, half:]
    g22 = jnp.where(i < j, mixed, flipped)
    g22 = jnp.where(i == j, diag2, g22)
    work2[...] = g22 * side2 * root2 - lax.dot_general(
        right, right, (((0,), (0,)), ((), ())),
        precision=EXACT, preferred_element_type=jnp.float32,
    )
    factor_rows(work2, upper2)
    size1, size2 = diag1 * root1, diag2 * root2
    out_ref[:half, :half] = jnp.where(i >= j, (upper1[:, :half] * size1).T, 0.0)
    out_ref[:half, half:] = jnp.zeros((half, half), jnp.float32)
    out_ref[half:, :half] = (right * size2).T
    out_ref[half:, half:] = jnp.where(i >= j, (upper2[...] * size2).T, 0.0)


def per_device(volume):
    packed = summed_gram(volume)
    half = packed.shape[2]
    vmem = pl.BlockSpec(memory_space=pltpu.VMEM)
    return pl.pallas_call(
        factor_kernel,
        out_shape=jax.ShapeDtypeStruct((2 * half, 2 * half), jnp.float32),
        in_specs=[vmem],
        out_specs=vmem,
        scratch_shapes=[
            pltpu.VMEM((half, 2 * half), jnp.float32),
            pltpu.VMEM((half, half), jnp.float32),
            pltpu.VMEM((half, 2 * half), jnp.float32),
            pltpu.VMEM((half, half), jnp.float32),
        ],
        compiler_params=pltpu.CompilerParams(vmem_limit_bytes=16 * 1024 * 1024),
        name="factor",
    )(packed)


def solution(mesh):
    return jax.shard_map(
        per_device,
        mesh=mesh,
        in_specs=(P("frame", "vox", None, None),),
        out_specs=P(),
        check_vma=False,
    )
```

```python
import functools

import jax
import jax.numpy as jnp
from jax import lax
from jax.experimental import pallas as pl
from jax.experimental.pallas import tpu as pltpu
from jax.sharding import PartitionSpec as P

MESH = pl.DeviceIdType.MESH
CORES = 2
EXACT = lax.Precision.HIGHEST
ROWS, LANES = 8, 128


def gram_kernel(
    frames, voxes, columns,
    vol_ref, out_ref,
    recv, block_ref, part, plane, line, total,
    a_send, a_recv, b_send, b_recv, c_send, c_recv, d_send, d_recv, own_sem,
):
    f = lax.axis_index("frame")
    v = lax.axis_index("vox")
    chip, core = v // CORES, v % CORES
    chips = voxes // CORES
    own = f * CORES + core
    members = frames * CORES
    rows_z, xd = vol_ref.shape[0], vol_ref.shape[2]
    half = rows_z * voxes // 2
    share = 2 * half // members

    def plane_peer(k):
        q = lax.rem(own + k, members)
        return q, (q // CORES, chip * CORES + q % CORES)

    def line_peer(k):
        c = lax.rem(chip + k, chips)
        return c, (f, c * CORES + core)

    barrier = pltpu.get_barrier_semaphore()
    for k in range(1, voxes):
        pl.semaphore_signal(
            barrier, inc=1, device_id=(f, lax.rem(v + k, voxes)), device_id_type=MESH
        )
    for k in range(1, members):
        pl.semaphore_signal(
            barrier, inc=1, device_id=plane_peer(k)[1], device_id_type=MESH
        )

    mine = pl.ds(v * rows_z, rows_z)
    stay = pltpu.make_async_copy(vol_ref.at[:, v], recv.at[mine], own_sem)
    stay.start()
    pl.semaphore_wait(barrier, voxes - 1 + members - 1)

    copies = []
    for k in sorted(range(1, voxes), key=lambda k: abs(k - voxes // 2)):
        p = lax.rem(v + k, voxes)
        copy = pltpu.make_async_remote_copy(
            src_ref=vol_ref.at[:, p],
            dst_ref=recv.at[mine],
            send_sem=a_send.at[k],
            recv_sem=a_recv.at[k],
            device_id=(f, p),
            device_id_type=MESH,
        )
        copy.start()
        copies.append((k, copy))
    def place(source):
        for x in range(xd):
            block_ref[source, :, x * LANES:(x + 1) * LANES] = recv[
                pl.ds(source * rows_z, rows_z), x, :
            ]

    stay.wait()
    place(v)
    for k, copy in reversed(copies):
        copy.wait_recv()
        place(lax.rem(v + voxes - k, voxes))
    block = block_ref[...].reshape(2 * half, xd * LANES)
    top, low = block[:half], block[half:]

    def dot(x, y):
        return lax.dot_general(
            x, y, (((1,), (1,)), ((), ())),
            precision=EXACT, preferred_element_type=jnp.float32,
        )

    def share_copy(q, landing):
        return pltpu.make_async_remote_copy(
            src_ref=part.at[q],
            dst_ref=plane.at[landing],
            send_sem=b_send.at[q],
            recv_sem=b_recv.at[landing],
            device_id=(q // CORES, chip * CORES + q % CORES),
            device_id_type=MESH,
        )

    def send_shares(first, rows, diag):
        for q in range(first, first + members // 2):
            row = (q - first) * share
            part[q, :share, :] = rows[row:row + share]
            part[q, share:, :] = diag

            @pl.when(q != own)
            def _():
                share_copy(q, own).start()

    i = lax.broadcasted_iota(jnp.int32, (half, half), 0)
    j = lax.broadcasted_iota(jnp.int32, (half, half), 1)
    send_shares(0, dot(low, top), jnp.zeros((1, half), jnp.float32))
    g22 = dot(low, low)
    diag = jnp.sum(jnp.where(i == j, g22, 0.0), axis=0, keepdims=True)
    send_shares(members // 2, jnp.where(i >= j, dot(top, top), g22), diag)
    plane[own] = part[own]
    for k, copy in copies:
        copy.wait_send()
    for q in range(members):
        @pl.when(q != own)
        def _():
            share_copy(q, q).wait()

    line[chip] = jnp.sum(plane[...], axis=0)
    copies = []
    for k in range(1, chips):
        c, device = line_peer(k)
        copy = pltpu.make_async_remote_copy(
            src_ref=line.at[chip],
            dst_ref=line.at[chip],
            send_sem=c_send.at[k],
            recv_sem=c_recv.at[k],
            device_id=device,
            device_id_type=MESH,
        )
        copy.start()
        copies.append(copy)
    for copy in copies:
        copy.wait()

    total[own] = jnp.sum(line[...], axis=0) / jnp.float32(columns)
    copies = []
    for k in range(1, members):
        q, device = plane_peer(k)
        copy = pltpu.make_async_remote_copy(
            src_ref=total.at[own],
            dst_ref=total.at[own],
            send_sem=d_send.at[k],
            recv_sem=d_recv.at[k],
            device_id=device,
            device_id_type=MESH,
        )
        copy.start()
        copies.append(copy)
    for copy in copies:
        copy.wait()
    out_ref[...] = total[...]


def summed_gram(volume):
    frames, voxes = lax.axis_size("frame"), lax.axis_size("vox")
    rows_z, rows_x, lanes = volume.shape[1:]
    columns = float(volume.shape[0] * frames * rows_x * lanes)
    xd = rows_x // voxes
    members = frames * CORES
    full = rows_z * voxes
    half = full // 2
    share = full // members
    packed = (members, share + 1, half)
    split = volume.reshape(rows_z, voxes, xd, lanes)
    dma = pltpu.SemaphoreType.DMA
    vmem = pl.BlockSpec(memory_space=pltpu.VMEM)
    return pl.pallas_call(
        functools.partial(gram_kernel, frames, voxes, columns),
        out_shape=jax.ShapeDtypeStruct(packed, jnp.float32),
        in_specs=[pl.BlockSpec(memory_space=pltpu.HBM)],
        out_specs=vmem,
        scratch_shapes=[
            pltpu.VMEM((full, xd, lanes), jnp.float32),
            pltpu.VMEM((voxes, rows_z, xd * lanes), jnp.float32),
            pltpu.VMEM(packed, jnp.float32),
            pltpu.VMEM(packed, jnp.float32),
            pltpu.VMEM((voxes // CORES, share + 1, half), jnp.float32),
            pltpu.VMEM(packed, jnp.float32),
            dma((voxes,)), dma((voxes,)),
            dma((members,)), dma((members,)),
            dma((voxes // CORES,)), dma((voxes // CORES,)),
            dma((members,)), dma((members,)),
            dma,
        ],
        compiler_params=pltpu.CompilerParams(
            collective_id=0, has_side_effects=True, vmem_limit_bytes=24 * 1024 * 1024
        ),
        name="summed_gram",
    )(pltpu.with_memory_space_constraint(split, pltpu.HBM))


def reciprocal(d):
    return pl.reciprocal(d, approx=True)


def splat_lane(rows, lane):
    return jnp.broadcast_to(rows[:, lane:lane + 1], (ROWS, LANES))


def splat_row(rows, i):
    return jnp.broadcast_to(rows[i:i + 1], rows.shape)


def factor_rows(work, upper):
    height, width = work.shape
    wide = lambda t: jnp.concatenate([t] * (width // LANES), axis=1)
    pairs = [(i, j) for j in range(ROWS) for i in range(j, ROWS)]
    panel = work[:ROWS, :]
    corner = [splat_lane(panel[:, :LANES], j) for j in range(ROWS)]
    for k in range(0, height, ROWS):
        last = k + ROWS == height
        s = {(i, j): splat_row(corner[j], i) for i, j in pairs}
        rows = [splat_row(panel, i) for i in range(ROWS)]
        if not last:
            panel = work[k + ROWS:k + 2 * ROWS, :]
            left = [splat_lane(panel[:, :LANES], k + j) for j in range(ROWS)]
            corner = [splat_lane(panel[:, :LANES], k + ROWS + j) for j in range(ROWS)]
        inv, low, pivot, scaled = [None] * ROWS, {}, [None] * ROWS, [None] * ROWS
        for m in range(0, ROWS, 2):
            n = m + 1
            a, b, c = s[m, m], s[n, m], s[n, n]
            det = a * c - b * b
            inv_det = reciprocal(det)
            inv[m] = reciprocal(a)
            inv[n] = a * inv_det
            pivot[m], pivot[n] = a, det * inv[m]
            low[n, m] = b * inv[m]
            second = {}
            for i in range(n + 1, ROWS):
                low[i, m] = s[i, m] * inv[m]
                second[i] = s[i, n] - low[i, m] * b
                low[i, n] = second[i] * inv[n]
            for i, j in pairs:
                if j <= n:
                    continue
                first = s[i, j] - low[i, m] * s[j, m]
                if i <= n + 2:
                    s[i, j] = first - (a * second[i] * second[j]) * inv_det
                else:
                    s[i, j] = first - low[i, n] * second[j]
            for q in (m, n):
                for i in range(q + 1, ROWS):
                    rows[i] = rows[i] - wide(low[i, q]) * rows[q]
                scaled[q] = rows[q] * wide(inv[q])
                if last:
                    continue
                for i in range(q + 1, ROWS):
                    left[i] = left[i] - low[i, q] * left[q]
                panel = panel - wide(left[q]) * scaled[q]
                turned = left[q] * inv[q]
                corner = [
                    corner[j] - left[q] * splat_row(turned, j) for j in range(ROWS)
                ]
        for i in range(ROWS):
            row = rows[i] * wide(lax.rsqrt(pivot[i]))
            upper[k + i:k + i + 1, :] = row[:1]
        if k + 2 * ROWS >= height:
            continue
        solved = list(scaled)
        for i in reversed(range(ROWS)):
            for m in reversed(range(i + 1, ROWS)):
                solved[i] = solved[i] - wide(low[m, i]) * solved[m]
        for g in range(k + 2 * ROWS, height, ROWS):
            group = work[g:g + ROWS, :]
            terms = [
                wide(splat_lane(group[:, :LANES], k + j)) * solved[j] for j in range(ROWS)
            ]
            while len(terms) > 1:
                terms = [x + y for x, y in zip(terms[::2], terms[1::2])]
            work[g:g + ROWS, :] = group - terms[0]


def factor_kernel(packed_ref, out_ref, work1, work2, upper1, upper2):
    members, rows, half = packed_ref.shape
    share = rows - 1
    main = [packed_ref[q, :share, :] for q in range(members)]
    g21 = jnp.concatenate(main[:members // 2], axis=0)
    mixed = jnp.concatenate(main[members // 2:], axis=0)
    i = lax.broadcasted_iota(jnp.int32, (half, half), 0)
    j = lax.broadcasted_iota(jnp.int32, (half, half), 1)
    diag1 = jnp.sum(jnp.where(i == j, mixed, 0.0), axis=0, keepdims=True)
    diag2 = packed_ref[members // 2, share:, :]
    root1, root2 = lax.rsqrt(diag1), lax.rsqrt(diag2)
    side1 = jnp.broadcast_to(root1, (half, half)).T
    side2 = jnp.broadcast_to(root2, (half, half)).T
    flipped = mixed.T
    work1[:, :half] = jnp.where(i >= j, mixed, flipped) * side1 * root1
    work1[:, half:] = g21.T * side1 * root2
    factor_rows(work1, upper1)
    right = upper1[:, half:]
    g22 = jnp.where(i < j, mixed, flipped)
    g22 = jnp.where(i == j, diag2, g22)
    work2[...] = g22 * side2 * root2 - lax.dot_general(
        right, right, (((0,), (0,)), ((), ())),
        precision=EXACT, preferred_element_type=jnp.float32,
    )
    factor_rows(work2, upper2)
    size1, size2 = diag1 * root1, diag2 * root2
    out_ref[:half, :half] = jnp.where(i >= j, (upper1[:, :half] * size1).T, 0.0)
    out_ref[:half, half:] = jnp.zeros((half, half), jnp.float32)
    out_ref[half:, :half] = (right * size2).T
    out_ref[half:, half:] = jnp.where(i >= j, (upper2[...] * size2).T, 0.0)


def per_device(volume):
    packed = summed_gram(volume)
    half = packed.shape[2]
    vmem = pl.BlockSpec(memory_space=pltpu.VMEM)
    return pl.pallas_call(
        factor_kernel,
        out_shape=jax.ShapeDtypeStruct((2 * half, 2 * half), jnp.float32),
        in_specs=[vmem],
        out_specs=vmem,
        scratch_shapes=[
            pltpu.VMEM((half, 2 * half), jnp.float32),
            pltpu.VMEM((half, half), jnp.float32),
            pltpu.VMEM((half, 2 * half), jnp.float32),
            pltpu.VMEM((half, half), jnp.float32),
        ],
        compiler_params=pltpu.CompilerParams(vmem_limit_bytes=16 * 1024 * 1024),
        name="factor",
    )(packed)


def solution(mesh):
    return jax.shard_map(
        per_device,
        mesh=mesh,
        in_specs=(P("frame", "vox", None, None),),
        out_specs=P(),
        check_vma=False,
    )
```
